32 devices in a mesh: tm: 4 (over x, core), pts: 8 (over z, y).
Axes of the slice: x: 2, y: 2, z: 4, core: 2. Of those that a mesh axis runs over, the one named last changes fastest.
Arguments:
- base_grid: float32 [12, 128, 8192], P(None, 'tm', 'pts'), may hold values from -5 to 5
- sample_index: int32 [4096], P('pts'), may hold values from 0 to 1023, as said below
- exponents: int32 [512, 12], replicated, may hold values from 0 to 3, as said below
Outputs:
- gram: float32 [512, 512], P('pts', 'tm')
- cross: float32 [3, 512], P(None, 'pts')
The draws below stay inside these ranges and needn't reach their ends.
Inputs may be any that keep to these rules, and one draw needn't show every extreme that they name: `sample_index`: within one index of pts the sampled cells are distinct, and each is below 1024. `exponents`: every term has total degree at most 3.
All inputs are finite; a program needn't handle non-finite values.
Results may differ from the reference program's by a relative error of at most 0.00034.
Values sent between devices are 32-bit elements; how exact they have to be, the bound alone decides.
A program may use at most 192 MiB of HBM per device.

```python
import jax
import jax.numpy as jnp
from jax import lax

TERMS = 512
FIELDS = 12
TARGETS = 3
PTS_DEV = 512
GRID_DEV = 1024
TIMES = 128
SAMPLES = 4096
CELLS = 8192
N_PTS = 8


def draw_sample_index(key, part):
    keys = jax.random.split(jax.random.fold_in(key, 11), N_PTS)

    def one_block(block_key):
        picked = jax.random.permutation(block_key, GRID_DEV - 1)[:PTS_DEV - 1].astype(jnp.int32)
        return jnp.concatenate([picked, jnp.array([GRID_DEV - 1], jnp.int32)])
    return jax.vmap(one_block)(keys).reshape(-1).astype(jnp.int32)


def draw_exponents(key, part):
    key_slots, key_live = jax.random.split(jax.random.fold_in(key, 23))
    slots = jax.random.randint(key_slots, (TERMS, 3), 0, FIELDS).astype(jnp.int32)
    live = (jax.random.randint(key_live, (TERMS, 3), 0, 4) > 0).astype(jnp.int32)
    forced = (jnp.arange(TERMS) % 64 == 0)[:, None]
    slots = jnp.where(forced, slots[:, :1], slots)
    live = jnp.where(forced, 1, live)
    hits = (slots[:, :, None] == jnp.arange(FIELDS)[None, None, :]).astype(jnp.int32)
    return jnp.sum(hits * live[:, :, None], axis=1).astype(jnp.int32)


def level_of(own_key, extent, cuts, smallest, top_value):
    def one(position, parts):
        steps = jax.random.uniform(jax.random.fold_in(jax.random.fold_in(own_key, 6), position), (parts,), jnp.float32, smallest / len(cuts), top_value / len(cuts))
        return jnp.repeat(jnp.exp(steps), extent[position] // parts).reshape((-1,) + (1,) * (len(extent) - position - 1))

    gain = one(*cuts[0])
    for cut in cuts[1:]:
        gain = gain * one(*cut)
    return gain


def normal_values(own_key, extent, deviation, limit, shards=(), dtype=jnp.bfloat16):
    drawn = jax.random.normal(own_key, extent, jnp.float32) * deviation
    if len(shards) > 0:
        drawn = level_of(own_key, extent, shards, -0.22, 0.18) * drawn
    return jnp.clip(drawn, min=-limit, max=limit).astype(dtype)


def setup_inputs(seed: int = 0) -> dict:
    splits = jax.random.split(jax.random.key(seed), 4)
    return {
        "base_grid": normal_values(splits[0], (FIELDS, TIMES, CELLS), 0.8, 5.0, ((1, 4), (2, 8)), jnp.float32),
        "sample_index": draw_sample_index(jax.random.fold_in(splits[3], 71), 0),
        "exponents": draw_exponents(jax.random.fold_in(splits[3], 71), 0),
    }


def monomials(piece, exponents):
    theta = jnp.ones((exponents.shape[0],) + piece.shape[1:], jnp.float32)
    for field in range(piece.shape[0]):
        value = piece[field][None]
        square = value * value
        power = exponents[:, field][:, None, None]
        factor = jnp.where(power == 0, jnp.float32(1.0), jnp.where(power == 1, value, jnp.where(power == 2, square, square * value)))
        theta = theta * factor
    return theta


def reference(base_grid, sample_index, exponents):
    owner = (jnp.arange(SAMPLES) // PTS_DEV).astype(jnp.int32)
    cells = (sample_index + owner * GRID_DEV).astype(jnp.int32)
    sampled = jnp.take(base_grid, cells, axis=2)
    width = min(64, SAMPLES)
    count = SAMPLES // width
    pieces = jnp.transpose(sampled.reshape(FIELDS, TIMES, count, width), (2, 0, 1, 3))
    scale = jnp.float32(1.0 / TIMES)

    def step(carry, piece):
        gram_acc, cross_acc = carry
        theta = monomials(piece, exponents)
        running = jnp.cumsum(theta, axis=1)
        before = jnp.concatenate([jnp.zeros_like(running[:, :1]), running[:, :-1]], axis=1)
        integral = (before * scale).astype(jnp.bfloat16).reshape(TERMS, TIMES * width)
        increment = (piece[:TARGETS] - piece[:TARGETS, :1]).astype(jnp.bfloat16).reshape(TARGETS, TIMES * width)
        gram_acc = gram_acc + jnp.dot(integral, integral.T, preferred_element_type=jnp.float32)
        cross_acc = cross_acc + jnp.dot(increment, integral.T, preferred_element_type=jnp.float32)
        return (gram_acc, cross_acc), None

    start = (jnp.zeros((TERMS, TERMS), jnp.float32), jnp.zeros((TARGETS, TERMS), jnp.float32))
    (gram_acc, cross_acc), unused = lax.scan(step, start, pieces)
    norm = jnp.float32(1.0 / (TIMES * SAMPLES))
    return gram_acc * norm, cross_acc * norm
```

```python
import itertools

import jax
import jax.numpy as jnp
import numpy as np
from jax import lax
from jax.experimental import pallas as pl
from jax.experimental.pallas import tpu as pltpu
from jax.sharding import PartitionSpec as P

LANES = 128
SLOTS = 16
TARGETS = 3
BLOCK = 8
F32 = jnp.float32
BF16 = jnp.bfloat16


def nt(a, b):
    return lax.dot_general(a, b, (((1,), (1,)), ((), ())), preferred_element_type=F32)


def split_two(value):
    high = value.astype(BF16)
    return high, (value - high.astype(F32)).astype(BF16)


def row_plan():
    plan, labels = [], []
    a_rows = {r: [(i + r) % 8 for i in range(8)] for r in range(8)}
    slot_var = [8, 9, 10, 11, 12, 8, 9, 10]
    b_rows = {r: [slot_var[(i + r) % 8] for i in range(8)] for r in range(8)}

    def add(kind, factors):
        plan.append(kind)
        labels.append([tuple(sorted(row)) for row in zip(*factors)])

    for r in range(5):
        for b in range(5):
            add(("aab", r, b), (a_rows[0], a_rows[r], [8 + b] * 8))
    for i in range(5):
        for j in range(i, 5):
            add(("abb", i, j), (a_rows[0], [8 + i] * 8, [8 + j] * 8))
    seen = set()
    for r in range(5):
        for s in range(8):
            rows = [tuple(sorted(row)) for row in zip(a_rows[0], a_rows[r], a_rows[s])]
            if not seen.intersection(rows):
                seen.update(rows)
                add(("aaa", r, s), (a_rows[0], a_rows[r], a_rows[s]))
    for i, j, k in ((0, 0, 0), (0, 0, 1), (0, 0, 2), (0, 0, 3), (1, 1, 0), (0, 1, 2), (0, 1, 3)):
        add(("bbb", i, j, k), (b_rows[i], b_rows[j], b_rows[k]))
    codes, known = [], set()
    for label in itertools.chain(*labels):
        fresh = label not in known
        known.add(label)
        codes.append(float(sum(4**v for v in label if v < 12)) if fresh else -1.0)
    assert len(known) == 455
    return plan, codes


PLAN, CODES = row_plan()
ROWS = 8 * len(PLAN)
FULL = -(-(ROWS + 8) // 16) * 16
HALF = FULL // 2


def sample(grid_ref, index_ref, out_ref):
    cells = grid_ref.shape[1]
    width = index_ref.shape[1]
    number = lax.broadcasted_iota(jnp.int32, (cells, width), 0)
    hot = jnp.where(number == index_ref[...], 1.0, 0.0).astype(BF16)
    value = grid_ref[...]
    high, rest = value.astype(BF16), None
    rest = value - high.astype(F32)
    middle, low = split_two(rest)
    out = jnp.dot(high, hot, preferred_element_type=F32)
    out += jnp.dot(middle, hot, preferred_element_type=F32)
    out += jnp.dot(low, hot, preferred_element_type=F32)
    for d in range(out_ref.shape[0]):
        out_ref[d] = out[:, d * LANES : (d + 1) * LANES]


def build(xs, first, run, integral, source, start, snaps):
    for sub in range(0, BLOCK, 4):
        steps = range(4)
        v, quad, wide = [], [], []
        for j in steps:
            t = start + sub + j
            v.append(xs[source, pl.ds(t, 8, stride=snaps), :])
            quad.append({})
            wide.append(
                [
                    jnp.broadcast_to(xs[source, pl.ds((8 + b) * snaps + t, 1), :], (8, LANES))
                    for b in range(5)
                ]
            )

        def rolled(j, r):
            return v[j] if r == 0 else pltpu.roll(v[j], 8 - r, 0)

        def pair(j, r):
            if r not in quad[j]:
                quad[j][r] = v[j] * rolled(j, r)
            return quad[j][r]

        def b_window(j, r):
            w = xs[source, pl.ds(8 * snaps + start + sub + j, 8, stride=snaps), :]
            return w if r == 0 else pltpu.roll(w, 8 - r, 0)

        def theta(kind, j):
            if kind[0] == "aab":
                return pair(j, kind[1]) * wide[j][kind[2]]
            if kind[0] == "abb":
                return (v[j] * wide[j][kind[1]]) * wide[j][kind[2]]
            if kind[0] == "aaa":
                return pair(j, kind[1]) * rolled(j, kind[2])
            return (b_window(j, kind[1]) * b_window(j, kind[2])) * b_window(j, kind[3])

        for g in range(0, len(PLAN), 2):
            rows = slice(8 * g, 8 * g + 16)
            now = run[rows, :]
            for j in steps:
                lanes = slice((sub + j) * LANES, (sub + j + 1) * LANES)
                integral[rows, lanes] = now.astype(BF16)
                now = now + jnp.concatenate([theta(PLAN[g], j), theta(PLAN[g + 1], j)], 0)
            run[rows, :] = now
        for j in steps:
            lanes = slice((sub + j) * LANES, (sub + j + 1) * LANES)
            change = v[j] - first
            both = jnp.concatenate([change, jnp.zeros_like(change)], 0)
            integral[ROWS : ROWS + 16, lanes] = both.astype(BF16)


def add_products(integral, g00, g01, g11):
    top, bottom = integral[:HALF, :], integral[HALF:, :]
    g00[...] += nt(top, top)
    g01[...] += nt(top, bottom)
    g11[...] += nt(bottom, bottom)


def chosen(exps_ref, codes_ref, g00, g01, g11):
    terms, fields = exps_ref.shape
    power = lax.broadcasted_iota(jnp.int32, (1, fields), 1)
    weight = lax.shift_left(jnp.int32(1), 2 * power).astype(F32)
    code = jnp.sum(exps_ref[...].astype(F32) * weight, axis=1, keepdims=True)
    pick = jnp.where(code == codes_ref[...], 1.0, 0.0).astype(BF16)
    upper = jnp.concatenate([g00[...], g01[...]], 1)
    lower = jnp.concatenate([g01[...].T, g11[...]], 1)
    gram = jnp.concatenate([upper, lower], 0)
    high, low = split_two(gram)
    by_row = jnp.dot(pick, high, preferred_element_type=F32)
    by_row += jnp.dot(pick, low, preferred_element_type=F32)
    high, low = split_two(by_row)
    out = nt(high, pick) + nt(low, pick)
    high, low = split_two(gram[ROWS : ROWS + 16, :])
    return out, nt(high, pick) + nt(low, pick)


def main(snaps, fields, x_ref, valid_ref, exps_ref, codes_ref, gram_ref, cross_ref,
         xs, run, i0, i1, g00, g01, g11):
    sources = x_ref.shape[0]
    for s in range(sources):
        xs[s, : fields * snaps, :] = x_ref[s]
        xs[s, fields * snaps : (fields + 1) * snaps, :] = jnp.broadcast_to(
            valid_ref[...], (snaps, LANES)
        )
        for k in range(3):
            to = (fields + 1 + k) * snaps
            xs[s, to : to + snaps, :] = x_ref[s, (8 + k) * snaps : (9 + k) * snaps, :]
    for ref in (run, g00, g01, g11, i1):
        ref[...] = jnp.zeros_like(ref)
    first = xs[0, pl.ds(0, 8, stride=snaps), :]
    per = snaps // BLOCK

    def two(number, carry):
        source = number // (per // 2)
        start = pl.multiple_of((number % (per // 2)) * 2 * BLOCK, 2 * BLOCK)
        build(xs, first, run, i0, source, start, snaps)
        add_products(i1, g00, g01, g11)
        build(xs, first, run, i1, source, start + BLOCK, snaps)
        add_products(i0, g00, g01, g11)
        return carry

    lax.fori_loop(0, sources * per // 2, two, 0)
    add_products(i1, g00, g01, g11)
    gram_ref[...], cross_ref[...] = chosen(exps_ref, codes_ref, g00, g01, g11)


def shards(base_grid, sample_index, exponents):
    fields, snaps, cells = base_grid.shape
    points = sample_index.shape[0]
    terms = exponents.shape[0]
    time_devices = lax.axis_size("tm")
    point_devices = lax.axis_size("pts")
    own = points // time_devices
    index = sample_index.reshape(time_devices, own)
    index = jnp.pad(index, ((0, 0), (0, LANES - own)), constant_values=-1)
    valid = jnp.where(jnp.arange(LANES) < own, 1.0, 0.0).astype(F32).reshape(1, LANES)
    codes = jnp.asarray(np.array(CODES + [-1.0] * (FULL - ROWS), np.float32)).reshape(1, FULL)
    sampled = pl.pallas_call(
        sample,
        out_shape=jax.ShapeDtypeStruct((time_devices, fields * snaps, LANES), F32),
        compiler_params=pltpu.CompilerParams(vmem_limit_bytes=50 << 20),
    )(base_grid.reshape(fields * snaps, cells), index.reshape(1, time_devices * LANES))
    received = lax.all_to_all(sampled, "tm", 0, 0)
    gram_part, cross_part = pl.pallas_call(
        lambda *refs: main(snaps, fields, *refs),
        out_shape=(
            jax.ShapeDtypeStruct((terms, terms), F32),
            jax.ShapeDtypeStruct((16, terms), F32),
        ),
        scratch_shapes=[
            pltpu.VMEM((time_devices, SLOTS * snaps, LANES), F32),
            pltpu.VMEM((ROWS, LANES), F32),
            pltpu.VMEM((FULL, BLOCK * LANES), BF16),
            pltpu.VMEM((FULL, BLOCK * LANES), BF16),
            pltpu.VMEM((HALF, HALF), F32),
            pltpu.VMEM((HALF, HALF), F32),
            pltpu.VMEM((HALF, HALF), F32),
        ],
        compiler_params=pltpu.CompilerParams(vmem_limit_bytes=50 << 20),
    )(received, valid, exponents, codes)
    scale = 1.0 / (snaps * time_devices)
    norm = 1.0 / (snaps * time_devices * points * point_devices)
    gram = lax.psum_scatter(gram_part, "tm", scatter_dimension=1, tiled=True)
    gram = lax.psum_scatter(gram, "pts", scatter_dimension=0, tiled=True)
    row_span = terms // point_devices
    cross = lax.psum(cross_part[:TARGETS], ("tm", "pts"))
    cross = lax.dynamic_slice_in_dim(cross, lax.axis_index("pts") * row_span, row_span, 1)
    return gram * jnp.float32(norm * scale * scale), cross * jnp.float32(norm * scale)


def solution(mesh):
    return jax.shard_map(
        shards,
        mesh=mesh,
        in_specs=(P(None, "tm", "pts"), P("pts"), P()),
        out_specs=(P("pts", "tm"), P(None, "pts")),
        check_vma=False,
    )
```

```python
import itertools

import jax
import jax.numpy as jnp
import numpy as np
from jax import lax
from jax.experimental import pallas as pl
from jax.experimental.pallas import tpu as pltpu
from jax.sharding import PartitionSpec as P

LANES = 128
SLOTS = 16
TARGETS = 3
BLOCK = 8
F32 = jnp.float32
BF16 = jnp.bfloat16


def nt(a, b):
    return lax.dot_general(a, b, (((1,), (1,)), ((), ())), preferred_element_type=F32)


def split_two(value):
    high = value.astype(BF16)
    return high, (value - high.astype(F32)).astype(BF16)


def row_plan():
    plan, labels = [], []
    a_rows = {r: [(i + r) % 8 for i in range(8)] for r in range(8)}
    slot_var = [8, 9, 10, 11, 12, 8, 9, 10]
    b_rows = {r: [slot_var[(i + r) % 8] for i in range(8)] for r in range(8)}

    def add(kind, factors):
        plan.append(kind)
        labels.append([tuple(sorted(row)) for row in zip(*factors)])

    for r in range(5):
        for b in range(5):
            add(("aab", r, b), (a_rows[0], a_rows[r], [8 + b] * 8))
    for i in range(5):
        for j in range(i, 5):
            add(("abb", i, j), (a_rows[0], [8 + i] * 8, [8 + j] * 8))
    seen = set()
    for r in range(5):
        for s in range(8):
            rows = [tuple(sorted(row)) for row in zip(a_rows[0], a_rows[r], a_rows[s])]
            if not seen.intersection(rows):
                seen.update(rows)
                add(("aaa", r, s), (a_rows[0], a_rows[r], a_rows[s]))
    for i, j, k in ((0, 0, 0), (0, 0, 1), (0, 0, 2), (0, 0, 3), (1, 1, 0), (0, 1, 2), (0, 1, 3)):
        add(("bbb", i, j, k), (b_rows[i], b_rows[j], b_rows[k]))
    codes, known = [], set()
    for label in itertools.chain(*labels):
        fresh = label not in known
        known.add(label)
        codes.append(float(sum(4**v for v in label if v < 12)) if fresh else -1.0)
    assert len(known) == 455
    return plan, codes


PLAN, CODES = row_plan()
ROWS = 8 * len(PLAN)
FULL = -(-(ROWS + 8) // 16) * 16
HALF = FULL // 2


def sample(grid_ref, index):
    number = lax.broadcasted_iota(jnp.int32, (grid_ref.shape[1], index.shape[1]), 0)
    hot = jnp.where(number == index, 1.0, 0.0).astype(BF16)
    value = grid_ref[...]
    high = value.astype(BF16)
    middle, low = split_two(value - high.astype(F32))
    out = jnp.dot(high, hot, preferred_element_type=F32)
    out += jnp.dot(middle, hot, preferred_element_type=F32)
    return out + jnp.dot(low, hot, preferred_element_type=F32)


def build(xs, first, run, integral, source, start, snaps):
    for sub in range(0, BLOCK, 4):
        steps = range(4)
        v, quad, wide = [], [], []
        for j in steps:
            t = start + sub + j
            v.append(xs[source, pl.ds(t, 8, stride=snaps), :])
            quad.append({})
            wide.append(
                [
                    jnp.broadcast_to(xs[source, pl.ds((8 + b) * snaps + t, 1), :], (8, LANES))
                    for b in range(5)
                ]
            )

        def rolled(j, r):
            return v[j] if r == 0 else pltpu.roll(v[j], 8 - r, 0)

        def pair(j, r):
            if r not in quad[j]:
                quad[j][r] = v[j] * rolled(j, r)
            return quad[j][r]

        def b_window(j, r):
            w = xs[source, pl.ds(8 * snaps + start + sub + j, 8, stride=snaps), :]
            return w if r == 0 else pltpu.roll(w, 8 - r, 0)

        def theta(kind, j):
            if kind[0] == "aab":
                return pair(j, kind[1]) * wide[j][kind[2]]
            if kind[0] == "abb":
                return (v[j] * wide[j][kind[1]]) * wide[j][kind[2]]
            if kind[0] == "aaa":
                return pair(j, kind[1]) * rolled(j, kind[2])
            return (b_window(j, kind[1]) * b_window(j, kind[2])) * b_window(j, kind[3])

        for g in range(0, len(PLAN), 2):
            rows = slice(8 * g, 8 * g + 16)
            now = run[rows, :]
            for j in steps:
                lanes = slice((sub + j) * LANES, (sub + j + 1) * LANES)
                integral[rows, lanes] = now.astype(BF16)
                now = now + jnp.concatenate([theta(PLAN[g], j), theta(PLAN[g + 1], j)], 0)
            run[rows, :] = now
        for j in steps:
            lanes = slice((sub + j) * LANES, (sub + j + 1) * LANES)
            change = v[j] - first
            both = jnp.concatenate([change, jnp.zeros_like(change)], 0)
            integral[ROWS : ROWS + 16, lanes] = both.astype(BF16)


def add_products(integral, g00, g01, g11):
    top, bottom = integral[:HALF, :], integral[HALF:, :]
    g00[...] += nt(top, top)
    g01[...] += nt(top, bottom)
    g11[...] += nt(bottom, bottom)


def choose(exps_ref, codes_ref, g00, g01, g11, part, rows, cols):
    terms, fields = exps_ref.shape
    cores, xs_, zs, ys = part.shape[:4]
    power = lax.broadcasted_iota(jnp.int32, (1, fields), 1)
    weight = lax.shift_left(jnp.int32(1), 2 * power).astype(F32)
    code = jnp.sum(exps_ref[...].astype(F32) * weight, axis=1, keepdims=True)
    pick = jnp.where(code == codes_ref[...], 1.0, 0.0).astype(BF16)
    upper = jnp.concatenate([g00[...], g01[...]], 1)
    lower = jnp.concatenate([g01[...].T, g11[...]], 1)
    gram = jnp.concatenate([upper, lower], 0)
    high, low = split_two(gram)
    by_row = jnp.dot(pick, high, preferred_element_type=F32)
    by_row += jnp.dot(pick, low, preferred_element_type=F32)
    high, low = split_two(by_row)
    out = nt(high, pick) + nt(low, pick)
    high, low = split_two(gram[ROWS : ROWS + 16, :])
    for p in range(zs * ys):
        own = pick[p * rows : (p + 1) * rows, :]
        cross = (nt(high, own) + nt(low, own))[:8]
        for c in range(cores * xs_):
            place = (c % cores, c // cores, p // ys, p % ys)
            block = out[p * rows : (p + 1) * rows, c * cols : (c + 1) * cols]
            part[place + (slice(0, rows), slice(0, cols))] = block
            part[place + (slice(rows, rows + 8), slice(0, rows))] = cross


class Exchange:
    def __init__(self, size, me, block, slots, sends, recvs, peer):
        self.size, self.me, self.block, self.slots = size, me, block, slots
        self.sends, self.recvs, self.peer = sends, recvs, peer

    def others(self):
        return [lax.rem(self.me + o, self.size) for o in range(1, self.size)]

    def copy(self, member, slot):
        return pltpu.make_async_remote_copy(
            src_ref=self.block(member),
            dst_ref=self.slots.at[slot],
            send_sem=self.sends.at[member],
            recv_sem=self.recvs.at[slot],
            device_id=self.peer(member),
            device_id_type=pl.DeviceIdType.MESH,
        )

    def start(self):
        for member in self.others():
            self.copy(member, self.me).start()

    def finish(self):
        total = self.block(self.me)[...]
        for member in self.others():
            self.copy(member, member).wait_recv()
            total = total + self.slots[member]
        return total

    def drain(self):
        for member in self.others():
            self.copy(member, member).wait_send()


def main(snaps, fields, shape, gram_norm, cross_norm,
         grid_ref, index_ref, valid_ref, exps_ref, codes_ref, gram_ref, cross_ref,
         samp, xs, run, i0, i1, g00, g01, g11, part, r_core, s0, r_ax, s_a1, r_ay, s_a2, r_az,
         r_by, s_b1, r_bx, s_b2, r_bz, sends, recvs, red_sends, red_recvs):
    chips, depth, tall = shape
    times = 2 * chips
    rows, cols = gram_ref.shape
    part_a = s_a1.shape[2]
    tm, pts = lax.axis_index("tm"), lax.axis_index("pts")
    x, core = tm // 2, lax.rem(tm, 2)
    z, y = pts // tall, lax.rem(pts, tall)
    mesh_id = pl.DeviceIdType.MESH

    barrier = pltpu.get_barrier_semaphore()
    for o in range(1, times):
        pl.semaphore_signal(barrier, inc=1, device_id=(lax.rem(tm + o, times), pts), device_id_type=mesh_id)
    for o in range(1, tall):
        pl.semaphore_signal(barrier, inc=1, device_id=(tm, z * tall + lax.rem(y + o, tall)), device_id_type=mesh_id)
    for o in range(1, depth):
        pl.semaphore_signal(barrier, inc=1, device_id=(tm, lax.rem(z + o, depth) * tall + y), device_id_type=mesh_id)
    pl.semaphore_wait(barrier, times - 1 + tall - 1 + depth - 1)

    live = fields * snaps

    def passed(to, source):
        return pltpu.make_async_remote_copy(
            src_ref=samp.at[to],
            dst_ref=xs.at[source, pl.ds(0, live)],
            send_sem=sends.at[to],
            recv_sem=recvs.at[source],
            device_id=(to, pts),
            device_id_type=mesh_id,
        )

    for o in range(1, chips + 1):
        there = lax.rem(x + o, chips)
        out = sample(grid_ref, index_ref[there])
        for c in range(2):
            samp[2 * there + c] = out[:, c * LANES : (c + 1) * LANES]
        if o < chips:
            for c in range(2):
                passed(2 * there + c, tm).start()
    passed(2 * x + 1 - core, tm).start()
    xs[tm, 0:live, :] = samp[tm]

    for ref in (run, g00, g01, g11, i1, part):
        ref[...] = jnp.zeros_like(ref)
    per = snaps // BLOCK

    def one_source(source, carry):
        @pl.when(source != tm)
        def _():
            passed(source, source).wait_recv()

        xs[source, live : live + snaps, :] = jnp.broadcast_to(valid_ref[...], (snaps, LANES))
        for k in range(3):
            to = (fields + 1 + k) * snaps
            xs[source, to : to + snaps, :] = xs[source, (8 + k) * snaps : (9 + k) * snaps, :]
        first = xs[0, pl.ds(0, 8, stride=snaps), :]

        def two(number, carry):
            start = pl.multiple_of(number * 2 * BLOCK, 2 * BLOCK)
            build(xs, first, run, i0, source, start, snaps)
            add_products(i1, g00, g01, g11)
            build(xs, first, run, i1, source, start + BLOCK, snaps)
            add_products(i0, g00, g01, g11)
            return carry

        return lax.fori_loop(0, per // 2, two, carry)

    lax.fori_loop(0, times, one_source, 0)
    add_products(i1, g00, g01, g11)
    for o in range(1, times):
        to = lax.rem(tm + o, times)
        passed(to, to).wait_send()
    choose(exps_ref, codes_ref, g00, g01, g11, part, rows, cols)

    def group(number, size, me, block, slots, peer):
        return Exchange(size, me, block, slots, red_sends.at[number], red_recvs.at[number], peer)

    def x_peer(j):
        return (2 * j + core, pts)

    def y_peer(j):
        return (tm, z * tall + j)

    def z_peer(j):
        return (tm, j * tall + y)

    e_core = group(0, 2, core, lambda j: part.at[j], r_core, lambda j: (2 * x + j, pts))
    e_ax = group(1, chips, x, lambda j: s0.at[j, :, :, 0:part_a], r_ax, x_peer)
    e_by = group(2, tall, y, lambda j: s0.at[:, :, j, part_a:], r_by, y_peer)
    e_ay = group(3, tall, y, lambda j: s_a1.at[:, j], r_ay, y_peer)
    e_bx = group(4, chips, x, lambda j: s_b1.at[j], r_bx, x_peer)
    e_az = group(5, depth, z, lambda j: s_a2.at[j], r_az, z_peer)
    e_bz = group(6, depth, z, lambda j: s_b2.at[j], r_bz, z_peer)
    e_core.start()
    s0[...] = e_core.finish()
    e_ax.start()
    e_by.start()
    s_a1[...] = e_ax.finish()
    e_ay.start()
    s_b1[...] = e_by.finish()
    e_bx.start()
    s_a2[...] = e_ay.finish()
    e_az.start()
    s_b2[...] = e_bx.finish()
    e_bz.start()
    top = e_az.finish()
    bottom = e_bz.finish()
    total = jnp.concatenate([top, bottom], 0)
    gram_ref[...] = total[:rows, :cols] * gram_norm
    cross_ref[...] = total[rows : rows + TARGETS, :rows] * cross_norm
    for exchange in (e_core, e_ax, e_by, e_ay, e_bx, e_az, e_bz):
        exchange.drain()


def shards(base_grid, sample_index, exponents):
    fields, snaps, cells = base_grid.shape
    points = sample_index.shape[0]
    terms = exponents.shape[0]
    times = lax.axis_size("tm")
    point_devices = lax.axis_size("pts")
    chips = times // 2
    depth = 4
    tall = point_devices // depth
    own = points // times
    index = sample_index.reshape(times, own)
    index = jnp.pad(index, ((0, 0), (0, LANES - own)), constant_values=-1)
    valid = jnp.where(jnp.arange(LANES) < own, 1.0, 0.0).astype(F32).reshape(1, LANES)
    codes = jnp.asarray(np.array(CODES + [-1.0] * (FULL - ROWS), np.float32)).reshape(1, FULL)
    scale = 1.0 / (snaps * times)
    norm = 1.0 / (snaps * times * points * point_devices)
    rows, cols = terms // point_devices, terms // times
    high = rows + 8
    part_a = -(-high // 16) * 8
    part_b = high - part_a

    def held(*extent):
        return pltpu.VMEM(extent + (LANES,), F32)

    most = max(chips, depth, tall, 2)
    return pl.pallas_call(
        lambda *refs: main(
            snaps, fields, (chips, depth, tall), norm * scale * scale, norm * scale, *refs
        ),
        out_shape=(
            jax.ShapeDtypeStruct((rows, cols), F32),
            jax.ShapeDtypeStruct((TARGETS, rows), F32),
        ),
        scratch_shapes=[
            held(times, fields * snaps),
            held(times, SLOTS * snaps),
            held(ROWS),
            pltpu.VMEM((FULL, BLOCK * LANES), BF16),
            pltpu.VMEM((FULL, BLOCK * LANES), BF16),
            pltpu.VMEM((HALF, HALF), F32),
            pltpu.VMEM((HALF, HALF), F32),
            pltpu.VMEM((HALF, HALF), F32),
            held(2, chips, depth, tall, high),
            held(2, chips, depth, tall, high),
            held(chips, depth, tall, high),
            held(chips, depth, tall, part_a),
            held(depth, tall, part_a),
            held(tall, depth, part_a),
            held(depth, part_a),
            held(depth, part_a),
            held(tall, chips, depth, part_b),
            held(chips, depth, part_b),
            held(chips, depth, part_b),
            held(depth, part_b),
            held(depth, part_b),
            pltpu.SemaphoreType.DMA((times,)),
            pltpu.SemaphoreType.DMA((times,)),
            pltpu.SemaphoreType.DMA((7, most)),
            pltpu.SemaphoreType.DMA((7, most)),
        ],
        compiler_params=pltpu.CompilerParams(
            collective_id=0, has_side_effects=True, vmem_limit_bytes=50 << 20
        ),
    )(
        base_grid.reshape(fields * snaps, cells),
        index.reshape(chips, 1, 2 * LANES),
        valid,
        exponents,
        codes,
    )


def solution(mesh):
    return jax.shard_map(
        shards,
        mesh=mesh,
        in_specs=(P(None, "tm", "pts"), P("pts"), P()),
        out_specs=(P("pts", "tm"), P(None, "pts")),
        check_vma=False,
    )
```

```python
import itertools

import jax
import jax.numpy as jnp
import numpy as np
from jax import lax
from jax.experimental import pallas as pl
from jax.experimental.pallas import tpu as pltpu
from jax.sharding import PartitionSpec as P

LANES = 128
SLOTS = 16
TARGETS = 3
BLOCK = 8
F32 = jnp.float32
BF16 = jnp.bfloat16


def nt(a, b):
    return lax.dot_general(a, b, (((1,), (1,)), ((), ())), preferred_element_type=F32)


def split_two(value):
    high = value.astype(BF16)
    return high, (value - high.astype(F32)).astype(BF16)


def row_plan():
    plan, labels = [], []
    a_rows = {r: [(i + r) % 8 for i in range(8)] for r in range(8)}
    slot_var = [8, 9, 10, 11, 12, 8, 9, 10]
    b_rows = {r: [slot_var[(i + r) % 8] for i in range(8)] for r in range(8)}

    def add(kind, factors):
        plan.append(kind)
        labels.append([tuple(sorted(row)) for row in zip(*factors)])

    for r in range(5):
        for b in range(5):
            add(("aab", r, b), (a_rows[0], a_rows[r], [8 + b] * 8))
    for i in range(5):
        for j in range(i, 5):
            add(("abb", i, j), (a_rows[0], [8 + i] * 8, [8 + j] * 8))
    seen = set()
    for r in range(5):
        for s in range(8):
            rows = [tuple(sorted(row)) for row in zip(a_rows[0], a_rows[r], a_rows[s])]
            if not seen.intersection(rows):
                seen.update(rows)
                add(("aaa", r, s), (a_rows[0], a_rows[r], a_rows[s]))
    for i, j, k in ((0, 0, 0), (0, 0, 1), (0, 0, 2), (0, 0, 3), (1, 1, 0), (0, 1, 2), (0, 1, 3)):
        add(("bbb", i, j, k), (b_rows[i], b_rows[j], b_rows[k]))
    codes, known = [], set()
    for label in itertools.chain(*labels):
        fresh = label not in known
        known.add(label)
        codes.append(float(sum(4**v for v in label if v < 12)) if fresh else -1.0)
    assert len(known) == 455
    return plan, codes


PLAN, CODES = row_plan()
ROWS = 8 * len(PLAN)
FULL = -(-(ROWS + 8) // 16) * 16
HALF = FULL // 2


def sample(grid_ref, index):
    number = lax.broadcasted_iota(jnp.int32, (grid_ref.shape[1], index.shape[1]), 0)
    hot = jnp.where(number == index, 1.0, 0.0).astype(BF16)
    value = grid_ref[...]
    high = value.astype(BF16)
    middle, low = split_two(value - high.astype(F32))
    out = jnp.dot(high, hot, preferred_element_type=F32)
    out += jnp.dot(middle, hot, preferred_element_type=F32)
    return out + jnp.dot(low, hot, preferred_element_type=F32)


def build(xs, first, run, integral, source, start, snaps):
    for sub in range(0, BLOCK, 4):
        steps = range(4)
        v, quad, wide = [], [], []
        for j in steps:
            t = start + sub + j
            v.append(xs[source, pl.ds(t, 8, stride=snaps), :])
            quad.append({})
            wide.append(
                [
                    jnp.broadcast_to(xs[source, pl.ds((8 + b) * snaps + t, 1), :], (8, LANES))
                    for b in range(5)
                ]
            )

        def rolled(j, r):
            return v[j] if r == 0 else pltpu.roll(v[j], 8 - r, 0)

        def pair(j, r):
            if r not in quad[j]:
                quad[j][r] = v[j] * rolled(j, r)
            return quad[j][r]

        def b_window(j, r):
            w = xs[source, pl.ds(8 * snaps + start + sub + j, 8, stride=snaps), :]
            return w if r == 0 else pltpu.roll(w, 8 - r, 0)

        def theta(kind, j):
            if kind[0] == "aab":
                return pair(j, kind[1]) * wide[j][kind[2]]
            if kind[0] == "abb":
                return (v[j] * wide[j][kind[1]]) * wide[j][kind[2]]
            if kind[0] == "aaa":
                return pair(j, kind[1]) * rolled(j, kind[2])
            return (b_window(j, kind[1]) * b_window(j, kind[2])) * b_window(j, kind[3])

        for g in range(0, len(PLAN), 2):
            rows = slice(8 * g, 8 * g + 16)
            now = run[rows, :]
            for j in steps:
                lanes = slice((sub + j) * LANES, (sub + j + 1) * LANES)
                integral[rows, lanes] = now.astype(BF16)
                now = now + jnp.concatenate([theta(PLAN[g], j), theta(PLAN[g + 1], j)], 0)
            run[rows, :] = now
        for j in steps:
            lanes = slice((sub + j) * LANES, (sub + j + 1) * LANES)
            change = v[j] - first
            both = jnp.concatenate([change, jnp.zeros_like(change)], 0)
            integral[ROWS : ROWS + 16, lanes] = both.astype(BF16)


def add_products(integral, g00, g01, g11):
    top, bottom = integral[:HALF, :], integral[HALF:, :]
    g00[...] += nt(top, top)
    g01[...] += nt(top, bottom)
    g11[...] += nt(bottom, bottom)


def choose(exps_ref, codes_ref, g00, g01, g11, part, rows, cols):
    fields, terms = exps_ref.shape
    cores, xs_, zs, ys = part.shape[:4]
    power = lax.broadcasted_iota(jnp.int32, (fields, 1), 0)
    weight = lax.shift_left(jnp.int32(1), 2 * power).astype(F32)
    code = jnp.sum(exps_ref[...].astype(F32) * weight, axis=0, keepdims=True)
    code = jnp.broadcast_to(code, (8, terms)).T[:, :1]
    pick = jnp.where(code == codes_ref[...], 1.0, 0.0).astype(BF16)
    upper = jnp.concatenate([g00[...], g01[...]], 1)
    lower = jnp.concatenate([g01[...].T, g11[...]], 1)
    gram = jnp.concatenate([upper, lower], 0)
    high, low = split_two(gram)
    by_row = jnp.dot(pick, high, preferred_element_type=F32)
    by_row += jnp.dot(pick, low, preferred_element_type=F32)
    high, low = split_two(by_row)
    out = nt(high, pick) + nt(low, pick)
    high, low = split_two(gram[ROWS : ROWS + 16, :])
    for p in range(zs * ys):
        own = pick[p * rows : (p + 1) * rows, :]
        cross = (nt(high, own) + nt(low, own))[:8]
        for c in range(cores * xs_):
            place = (c % cores, c // cores, p // ys, p % ys)
            block = out[p * rows : (p + 1) * rows, c * cols : (c + 1) * cols]
            part[place + (slice(0, rows), slice(0, cols))] = block
            part[place + (slice(rows, rows + 8), slice(0, rows))] = cross


class Exchange:
    def __init__(self, size, me, block, slots, sends, recvs, peer):
        self.size, self.me, self.block, self.slots = size, me, block, slots
        self.sends, self.recvs, self.peer = sends, recvs, peer

    def others(self):
        return [lax.rem(self.me + o, self.size) for o in range(1, self.size)]

    def copy(self, member, slot):
        return pltpu.make_async_remote_copy(
            src_ref=self.block(member),
            dst_ref=self.slots.at[slot],
            send_sem=self.sends.at[member],
            recv_sem=self.recvs.at[slot],
            device_id=self.peer(member),
            device_id_type=pl.DeviceIdType.MESH,
        )

    def start(self):
        for member in self.others():
            self.copy(member, self.me).start()

    def finish(self):
        total = self.block(self.me)[...]
        for member in self.others():
            self.copy(member, member).wait_recv()
            total = total + self.slots[member]
        return total

    def drain(self):
        for member in self.others():
            self.copy(member, member).wait_send()


def main(snaps, fields, own, shape, gram_norm, cross_norm,
         grid_in, index_in, exps_in, codes_in, gram_ref, cross_ref,
         grid_ref, index_ref, exps_ref, codes_ref, loads, samp, xs, run, i0, i1, g00, g01, g11, part, r_core, s0, r_ax, s_a1, r_ay, s_a2, r_az,
         r_by, s_b1, r_bx, s_b2, r_bz, sends, recvs, red_sends, red_recvs):
    chips, depth, tall = shape
    times = 2 * chips
    rows, cols = gram_ref.shape
    part_a = s_a1.shape[2]
    tm, pts = lax.axis_index("tm"), lax.axis_index("pts")
    x, core = tm // 2, lax.rem(tm, 2)
    z, y = pts // tall, lax.rem(pts, tall)
    mesh_id = pl.DeviceIdType.MESH

    pairs = ((grid_in, grid_ref), (index_in, index_ref), (exps_in, exps_ref), (codes_in, codes_ref))
    inputs = [pltpu.make_async_copy(a, b, loads.at[i]) for i, (a, b) in enumerate(pairs)]
    for copy in inputs:
        copy.start()
    barrier = pltpu.get_barrier_semaphore()
    for o in range(1, times):
        pl.semaphore_signal(barrier, inc=1, device_id=(lax.rem(tm + o, times), pts), device_id_type=mesh_id)
    for o in range(1, tall):
        pl.semaphore_signal(barrier, inc=1, device_id=(tm, z * tall + lax.rem(y + o, tall)), device_id_type=mesh_id)
    for o in range(1, depth):
        pl.semaphore_signal(barrier, inc=1, device_id=(tm, lax.rem(z + o, depth) * tall + y), device_id_type=mesh_id)
    pl.semaphore_wait(barrier, times - 1 + tall - 1 + depth - 1)

    live = fields * snaps
    inputs[1].wait()
    inputs[0].wait()

    def passed(to, source):
        return pltpu.make_async_remote_copy(
            src_ref=samp.at[to],
            dst_ref=xs.at[source, pl.ds(0, live)],
            send_sem=sends.at[to],
            recv_sem=recvs.at[source],
            device_id=(to, pts),
            device_id_type=mesh_id,
        )

    for o in range(1, chips + 1):
        there = lax.rem(x + o, chips)
        out = sample(grid_ref, index_ref[there])
        for c in range(2):
            samp[2 * there + c] = out[:, c * LANES : (c + 1) * LANES]
        if o < chips:

            @pl.when(core == 0)
            def _():
                for c in range(2):
                    passed(2 * there + c, tm).start()

    passed(2 * x + 1 - core, tm).start()
    xs[tm, 0:live, :] = samp[tm]

    for ref in (run, g00, g01, g11, i1, part):
        ref[...] = jnp.zeros_like(ref)
    per = snaps // BLOCK

    valid = jnp.where(lax.broadcasted_iota(jnp.int32, (snaps, LANES), 1) < own, 1.0, 0.0).astype(F32)

    def one_source(source, carry):
        @pl.when((source == 1) & (core == 1))
        def _():
            for o in range(1, chips):
                there = lax.rem(x + o, chips)
                for c in range(2):
                    passed(2 * there + c, tm).start()

        @pl.when(source != tm)
        def _():
            passed(source, source).wait_recv()

        xs[source, live : live + snaps, :] = valid
        for k in range(3):
            to = (fields + 1 + k) * snaps
            xs[source, to : to + snaps, :] = xs[source, (8 + k) * snaps : (9 + k) * snaps, :]
        first = xs[0, pl.ds(0, 8, stride=snaps), :]

        def two(number, carry):
            start = pl.multiple_of(number * 2 * BLOCK, 2 * BLOCK)
            build(xs, first, run, i0, source, start, snaps)
            add_products(i1, g00, g01, g11)
            build(xs, first, run, i1, source, start + BLOCK, snaps)
            add_products(i0, g00, g01, g11)
            return carry

        return lax.fori_loop(0, per // 2, two, carry)

    lax.fori_loop(0, times, one_source, 0)
    add_products(i1, g00, g01, g11)
    for o in range(1, times):
        to = lax.rem(tm + o, times)
        passed(to, to).wait_send()
    inputs[2].wait()
    inputs[3].wait()
    choose(exps_ref, codes_ref, g00, g01, g11, part, rows, cols)

    def group(number, size, me, block, slots, peer):
        return Exchange(size, me, block, slots, red_sends.at[number], red_recvs.at[number], peer)

    def x_peer(j):
        return (2 * j + core, pts)

    def y_peer(j):
        return (tm, z * tall + j)

    def z_peer(j):
        return (tm, j * tall + y)

    e_core = group(0, 2, core, lambda j: part.at[j], r_core, lambda j: (2 * x + j, pts))
    e_ax = group(1, chips, x, lambda j: s0.at[j, :, :, 0:part_a], r_ax, x_peer)
    e_by = group(2, tall, y, lambda j: s0.at[:, :, j, part_a:], r_by, y_peer)
    e_ay = group(3, tall, y, lambda j: s_a1.at[:, j], r_ay, y_peer)
    e_bx = group(4, chips, x, lambda j: s_b1.at[j], r_bx, x_peer)
    e_az = group(5, depth, z, lambda j: s_a2.at[j], r_az, z_peer)
    e_bz = group(6, depth, z, lambda j: s_b2.at[j], r_bz, z_peer)
    e_core.start()
    s0[...] = e_core.finish()
    e_ax.start()
    e_by.start()
    s_a1[...] = e_ax.finish()
    e_ay.start()
    s_b1[...] = e_by.finish()
    e_bx.start()
    s_a2[...] = e_ay.finish()
    e_az.start()
    s_b2[...] = e_bx.finish()
    e_bz.start()
    top = e_az.finish()
    bottom = e_bz.finish()
    total = jnp.concatenate([top, bottom], 0)
    gram_ref[...] = total[:rows, :cols] * gram_norm
    cross_ref[...] = total[rows : rows + TARGETS, :rows] * cross_norm
    for exchange in (e_core, e_ax, e_by, e_ay, e_bx, e_az, e_bz):
        exchange.drain()


def shards(base_grid, sample_index, exponents):
    fields, snaps, cells = base_grid.shape
    points = sample_index.shape[0]
    terms = exponents.shape[0]
    times = lax.axis_size("tm")
    point_devices = lax.axis_size("pts")
    chips = times // 2
    depth = 4
    tall = point_devices // depth
    own = points // times
    index = sample_index.reshape(times, own)
    index = jnp.pad(index, ((0, 0), (0, LANES - own)), constant_values=-1)
    codes = jnp.asarray(np.array(CODES + [-1.0] * (FULL - ROWS), np.float32)).reshape(1, FULL)
    scale = 1.0 / (snaps * times)
    norm = 1.0 / (snaps * times * points * point_devices)
    rows, cols = terms // point_devices, terms // times
    high = rows + 8
    part_a = -(-high // 16) * 8
    part_b = high - part_a

    def held(*extent):
        return pltpu.VMEM(extent + (LANES,), F32)

    most = max(chips, depth, tall, 2)
    return pl.pallas_call(
        lambda *refs: main(
            snaps, fields, own, (chips, depth, tall), norm * scale * scale, norm * scale, *refs
        ),
        out_shape=(
            jax.ShapeDtypeStruct((rows, cols), F32),
            jax.ShapeDtypeStruct((TARGETS, rows), F32),
        ),
        in_specs=[pl.BlockSpec(memory_space=pltpu.HBM)] * 4,
        scratch_shapes=[
            pltpu.VMEM((fields * snaps, cells), F32),
            pltpu.VMEM((chips, 1, 2 * LANES), jnp.int32),
            pltpu.VMEM((fields, terms), jnp.int32),
            pltpu.VMEM((1, FULL), F32),
            pltpu.SemaphoreType.DMA((4,)),
            held(times, fields * snaps),
            held(times, SLOTS * snaps),
            held(ROWS),
            pltpu.VMEM((FULL, BLOCK * LANES), BF16),
            pltpu.VMEM((FULL, BLOCK * LANES), BF16),
            pltpu.VMEM((HALF, HALF), F32),
            pltpu.VMEM((HALF, HALF), F32),
            pltpu.VMEM((HALF, HALF), F32),
            held(2, chips, depth, tall, high),
            held(2, chips, depth, tall, high),
            held(chips, depth, tall, high),
            held(chips, depth, tall, part_a),
            held(depth, tall, part_a),
            held(tall, depth, part_a),
            held(depth, part_a),
            held(depth, part_a),
            held(tall, chips, depth, part_b),
            held(chips, depth, part_b),
            held(chips, depth, part_b),
            held(depth, part_b),
            held(depth, part_b),
            pltpu.SemaphoreType.DMA((times,)),
            pltpu.SemaphoreType.DMA((times,)),
            pltpu.SemaphoreType.DMA((7, most)),
            pltpu.SemaphoreType.DMA((7, most)),
        ],
        compiler_params=pltpu.CompilerParams(
            collective_id=0, has_side_effects=True, vmem_limit_bytes=64 << 20
        ),
    )(
        base_grid.reshape(fields * snaps, cells),
        index.reshape(chips, 1, 2 * LANES),
        exponents.T,
        codes,
    )


def solution(mesh):
    return jax.shard_map(
        shards,
        mesh=mesh,
        in_specs=(P(None, "tm", "pts"), P("pts"), P()),
        out_specs=(P("pts", "tm"), P(None, "pts")),
        check_vma=False,
    )
```

```python
import itertools

import jax
import jax.numpy as jnp
import numpy as np
from jax import lax
from jax.experimental import pallas as pl
from jax.experimental.pallas import tpu as pltpu
from jax.sharding import PartitionSpec as P

LANES = 128
SLOTS = 16
TARGETS = 3
BLOCK = 8
F32 = jnp.float32
BF16 = jnp.bfloat16


def nt(a, b):
    return lax.dot_general(a, b, (((1,), (1,)), ((), ())), preferred_element_type=F32)


def split_two(value):
    high = value.astype(BF16)
    return high, (value - high.astype(F32)).astype(BF16)


def row_plan():
    plan, labels = [], []
    a_rows = {r: [(i + r) % 8 for i in range(8)] for r in range(8)}
    slot_var = [8, 9, 10, 11, 12, 8, 9, 10]
    b_rows = {r: [slot_var[(i + r) % 8] for i in range(8)] for r in range(8)}

    def add(kind, factors):
        plan.append(kind)
        labels.append([tuple(sorted(row)) for row in zip(*factors)])

    for r in range(5):
        for b in range(5):
            add(("aab", r, b), (a_rows[0], a_rows[r], [8 + b] * 8))
    for i in range(5):
        for j in range(i, 5):
            add(("abb", i, j), (a_rows[0], [8 + i] * 8, [8 + j] * 8))
    seen = set()
    for r in range(5):
        for s in range(8):
            rows = [tuple(sorted(row)) for row in zip(a_rows[0], a_rows[r], a_rows[s])]
            if not seen.intersection(rows):
                seen.update(rows)
                add(("aaa", r, s), (a_rows[0], a_rows[r], a_rows[s]))
    for i, j, k in ((0, 0, 0), (0, 0, 1), (0, 0, 2), (0, 0, 3), (1, 1, 0), (0, 1, 2), (0, 1, 3)):
        add(("bbb", i, j, k), (b_rows[i], b_rows[j], b_rows[k]))
    codes, known = [], set()
    for label in itertools.chain(*labels):
        fresh = label not in known
        known.add(label)
        codes.append(float(sum(4**v for v in label if v < 12)) if fresh else -1.0)
    assert len(known) == 455
    return plan, codes


PLAN, CODES = row_plan()
ROWS = 8 * len(PLAN)
FULL = -(-(ROWS + 8) // 16) * 16
HALF = FULL // 2


def sample(grid_ref, index):
    number = lax.broadcasted_iota(jnp.int32, (grid_ref.shape[1], index.shape[1]), 0)
    hot = jnp.where(number == index, 1.0, 0.0).astype(BF16)
    value = grid_ref[...]
    high = value.astype(BF16)
    middle, low = split_two(value - high.astype(F32))
    out = jnp.dot(high, hot, preferred_element_type=F32)
    out += jnp.dot(middle, hot, preferred_element_type=F32)
    return out + jnp.dot(low, hot, preferred_element_type=F32)


def build(xs, first, run, integral, source, start, snaps):
    for sub in range(0, BLOCK, 4):
        steps = range(4)
        v, quad, wide = [], [], []
        for j in steps:
            t = start + sub + j
            v.append(xs[source, pl.ds(t, 8, stride=snaps), :])
            quad.append({})
            wide.append(
                [
                    jnp.broadcast_to(xs[source, pl.ds((8 + b) * snaps + t, 1), :], (8, LANES))
                    for b in range(5)
                ]
            )

        def rolled(j, r):
            return v[j] if r == 0 else pltpu.roll(v[j], 8 - r, 0)

        def pair(j, r):
            if r not in quad[j]:
                quad[j][r] = v[j] * rolled(j, r)
            return quad[j][r]

        def b_window(j, r):
            w = xs[source, pl.ds(8 * snaps + start + sub + j, 8, stride=snaps), :]
            return w if r == 0 else pltpu.roll(w, 8 - r, 0)

        def theta(kind, j):
            if kind[0] == "aab":
                return pair(j, kind[1]) * wide[j][kind[2]]
            if kind[0] == "abb":
                return (v[j] * wide[j][kind[1]]) * wide[j][kind[2]]
            if kind[0] == "aaa":
                return pair(j, kind[1]) * rolled(j, kind[2])
            return (b_window(j, kind[1]) * b_window(j, kind[2])) * b_window(j, kind[3])

        for g in range(0, len(PLAN), 2):
            rows = slice(8 * g, 8 * g + 16)
            now = run[rows, :]
            for j in steps:
                lanes = slice((sub + j) * LANES, (sub + j + 1) * LANES)
                integral[rows, lanes] = now.astype(BF16)
                now = now + jnp.concatenate([theta(PLAN[g], j), theta(PLAN[g + 1], j)], 0)
            run[rows, :] = now
        for j in steps:
            lanes = slice((sub + j) * LANES, (sub + j + 1) * LANES)
            change = v[j] - first
            both = jnp.concatenate([change, jnp.zeros_like(change)], 0)
            integral[ROWS : ROWS + 16, lanes] = both.astype(BF16)


def add_products(integral, g00, g01, g11):
    top, bottom = integral[:HALF, :], integral[HALF:, :]
    g00[...] += nt(top, top)
    g01[...] += nt(top, bottom)
    g11[...] += nt(bottom, bottom)


def choose(exps_ref, codes_ref, g00, g01, g11, part, rows, cols):
    fields, terms = exps_ref.shape
    cores, xs_, zs, ys = part.shape[:4]
    power = lax.broadcasted_iota(jnp.int32, (fields, 1), 0)
    weight = lax.shift_left(jnp.int32(1), 2 * power).astype(F32)
    code = jnp.sum(exps_ref[...].astype(F32) * weight, axis=0, keepdims=True)
    code = jnp.broadcast_to(code, (8, terms)).T[:, :1]
    pick = jnp.where(code == codes_ref[...], 1.0, 0.0).astype(BF16)
    upper = jnp.concatenate([g00[...], g01[...]], 1)
    lower = jnp.concatenate([g01[...].T, g11[...]], 1)
    gram = jnp.concatenate([upper, lower], 0)
    high, low = split_two(gram)
    by_row = jnp.dot(pick, high, preferred_element_type=F32)
    by_row += jnp.dot(pick, low, preferred_element_type=F32)
    high, low = split_two(by_row)
    out = nt(high, pick) + nt(low, pick)
    high, low = split_two(gram[ROWS : ROWS + 16, :])
    for p in range(zs * ys):
        own = pick[p * rows : (p + 1) * rows, :]
        cross = (nt(high, own) + nt(low, own))[:8]
        for c in range(cores * xs_):
            place = (c % cores, c // cores, p // ys, p % ys)
            block = out[p * rows : (p + 1) * rows, c * cols : (c + 1) * cols]
            part[place + (slice(0, rows), slice(0, cols))] = block
            part[place + (slice(rows, rows + 8), slice(0, rows))] = cross


class Exchange:
    def __init__(self, size, me, block, slots, sends, recvs, peer):
        self.size, self.me, self.block, self.slots = size, me, block, slots
        self.sends, self.recvs, self.peer = sends, recvs, peer

    def others(self):
        return [lax.rem(self.me + o, self.size) for o in range(1, self.size)]

    def copy(self, member, slot):
        return pltpu.make_async_remote_copy(
            src_ref=self.block(member),
            dst_ref=self.slots.at[slot],
            send_sem=self.sends.at[member],
            recv_sem=self.recvs.at[slot],
            device_id=self.peer(member),
            device_id_type=pl.DeviceIdType.MESH,
        )

    def start(self):
        for member in self.others():
            self.copy(member, self.me).start()

    def finish(self):
        total = self.block(self.me)[...]
        for member in self.others():
            self.copy(member, member).wait_recv()
            total = total + self.slots[member]
        return total

    def drain(self):
        for member in self.others():
            self.copy(member, member).wait_send()


def main(snaps, fields, own, shape, gram_norm, cross_norm,
         grid_in, index_in, exps_in, codes_in, gram_ref, cross_ref,
         grid_ref, index_ref, exps_ref, codes_ref, loads, samp, xs, run, i0, i1, g00, g01, g11, part, r_core, s0, r_ax, s_a1, r_ay, s_a2, r_az,
         r_by, s_b1, r_bx, s_b2, r_bz, sends, recvs, red_sends, red_recvs):
    chips, depth, tall = shape
    times = 2 * chips
    rows, cols = gram_ref.shape
    part_a = s_a1.shape[2]
    tm, pts = lax.axis_index("tm"), lax.axis_index("pts")
    x, core = tm // 2, lax.rem(tm, 2)
    z, y = pts // tall, lax.rem(pts, tall)
    mesh_id = pl.DeviceIdType.MESH

    pairs = ((grid_in, grid_ref), (index_in, index_ref), (exps_in, exps_ref), (codes_in, codes_ref))
    inputs = [pltpu.make_async_copy(a, b, loads.at[i]) for i, (a, b) in enumerate(pairs)]
    for copy in inputs:
        copy.start()
    barrier = pltpu.get_barrier_semaphore()
    for o in range(1, times):
        pl.semaphore_signal(barrier, inc=1, device_id=(lax.rem(tm + o, times), pts), device_id_type=mesh_id)
    for o in range(1, tall):
        pl.semaphore_signal(barrier, inc=1, device_id=(tm, z * tall + lax.rem(y + o, tall)), device_id_type=mesh_id)
    for o in range(1, depth):
        pl.semaphore_signal(barrier, inc=1, device_id=(tm, lax.rem(z + o, depth) * tall + y), device_id_type=mesh_id)
    pl.semaphore_wait(barrier, times - 1 + tall - 1 + depth - 1)

    live = fields * snaps
    inputs[1].wait()
    inputs[0].wait()

    def passed(to, source):
        return pltpu.make_async_remote_copy(
            src_ref=samp.at[to],
            dst_ref=xs.at[source, pl.ds(0, live)],
            send_sem=sends.at[to],
            recv_sem=recvs.at[source],
            device_id=(to, pts),
            device_id_type=mesh_id,
        )

    for o in range(1, chips + 1):
        there = lax.rem(x + o, chips)
        out = sample(grid_ref, index_ref[there])
        for c in range(2):
            samp[2 * there + c] = out[:, c * LANES : (c + 1) * LANES]
        if o < chips:

            @pl.when(core == 0)
            def _():
                for c in range(2):
                    passed(2 * there + c, tm).start()

    passed(2 * x + 1 - core, tm).start()
    xs[tm, 0:live, :] = samp[tm]

    for ref in (run, g00, g01, g11, i1, part):
        ref[...] = jnp.zeros_like(ref)
    per = snaps // BLOCK

    valid = jnp.where(lax.broadcasted_iota(jnp.int32, (snaps, LANES), 1) < own, 1.0, 0.0).astype(F32)

    def one_source(source, carry):
        @pl.when((source == 1) & (core == 1))
        def _():
            for o in range(1, chips):
                there = lax.rem(x + o, chips)
                for c in range(2):
                    passed(2 * there + c, tm).start()

        @pl.when(source != tm)
        def _():
            passed(source, source).wait_recv()

        xs[source, live : live + snaps, :] = valid
        for k in range(3):
            to = (fields + 1 + k) * snaps
            xs[source, to : to + snaps, :] = xs[source, (8 + k) * snaps : (9 + k) * snaps, :]
        first = xs[0, pl.ds(0, 8, stride=snaps), :]

        def two(number, carry):
            start = pl.multiple_of(number * 2 * BLOCK, 2 * BLOCK)
            build(xs, first, run, i0, source, start, snaps)
            add_products(i1, g00, g01, g11)
            build(xs, first, run, i1, source, start + BLOCK, snaps)
            add_products(i0, g00, g01, g11)
            return carry

        return lax.fori_loop(0, per // 2, two, carry)

    lax.fori_loop(0, times, one_source, 0)
    add_products(i1, g00, g01, g11)
    for o in range(1, times):
        to = lax.rem(tm + o, times)
        passed(to, to).wait_send()
    inputs[2].wait()
    inputs[3].wait()
    choose(exps_ref, codes_ref, g00, g01, g11, part, rows, cols)

    def group(number, size, me, block, slots, peer):
        return Exchange(size, me, block, slots, red_sends.at[number], red_recvs.at[number], peer)

    def x_peer(j):
        return (2 * j + core, pts)

    def y_peer(j):
        return (tm, z * tall + j)

    def z_peer(j):
        return (tm, j * tall + y)

    def core_peer(j):
        return (2 * x + j, pts)

    upper, lower = slice(0, part_a), slice(part_a, part.shape[4])
    e_ca = group(0, 2, core, lambda j: part.at[j, :, :, :, upper], r_core.at[:, :, :, :, upper], core_peer)
    e_cb = group(7, 2, core, lambda j: part.at[j, :, :, :, lower], r_core.at[:, :, :, :, lower], core_peer)
    e_ax = group(1, chips, x, lambda j: s0.at[j, :, :, 0:part_a], r_ax, x_peer)
    e_by = group(2, tall, y, lambda j: s0.at[:, :, j, part_a:], r_by, y_peer)
    e_ay = group(3, tall, y, lambda j: s_a1.at[:, j], r_ay, y_peer)
    e_bx = group(4, chips, x, lambda j: s_b1.at[j], r_bx, x_peer)
    e_az = group(5, depth, z, lambda j: s_a2.at[j], r_az, z_peer)
    e_bz = group(6, depth, z, lambda j: s_b2.at[j], r_bz, z_peer)
    e_ca.start()
    e_cb.start()
    s0[:, :, :, upper] = e_ca.finish()
    e_ax.start()
    s0[:, :, :, lower] = e_cb.finish()
    e_by.start()
    s_a1[...] = e_ax.finish()
    e_ay.start()
    s_b1[...] = e_by.finish()
    e_bx.start()
    s_a2[...] = e_ay.finish()
    e_az.start()
    s_b2[...] = e_bx.finish()
    e_bz.start()
    top = e_az.finish()
    bottom = e_bz.finish()
    total = jnp.concatenate([top, bottom], 0)
    gram_ref[...] = total[:rows, :cols] * gram_norm
    cross_ref[...] = total[rows : rows + TARGETS, :rows] * cross_norm
    for exchange in (e_ca, e_cb, e_ax, e_by, e_ay, e_bx, e_az, e_bz):
        exchange.drain()


def shards(base_grid, sample_index, exponents):
    fields, snaps, cells = base_grid.shape
    points = sample_index.shape[0]
    terms = exponents.shape[0]
    times = lax.axis_size("tm")
    point_devices = lax.axis_size("pts")
    chips = times // 2
    depth = 4
    tall = point_devices // depth
    own = points // times
    index = sample_index.reshape(times, own)
    index = jnp.pad(index, ((0, 0), (0, LANES - own)), constant_values=-1)
    codes = jnp.asarray(np.array(CODES + [-1.0] * (FULL - ROWS), np.float32)).reshape(1, FULL)
    scale = 1.0 / (snaps * times)
    norm = 1.0 / (snaps * times * points * point_devices)
    rows, cols = terms // point_devices, terms // times
    high = rows + 8
    part_a = -(-high // 16) * 8
    part_b = high - part_a

    def held(*extent):
        return pltpu.VMEM(extent + (LANES,), F32)

    most = max(chips, depth, tall, 2)
    return pl.pallas_call(
        lambda *refs: main(
            snaps, fields, own, (chips, depth, tall), norm * scale * scale, norm * scale, *refs
        ),
        out_shape=(
            jax.ShapeDtypeStruct((rows, cols), F32),
            jax.ShapeDtypeStruct((TARGETS, rows), F32),
        ),
        in_specs=[pl.BlockSpec(memory_space=pltpu.HBM)] * 4,
        scratch_shapes=[
            pltpu.VMEM((fields * snaps, cells), F32),
            pltpu.VMEM((chips, 1, 2 * LANES), jnp.int32),
            pltpu.VMEM((fields, terms), jnp.int32),
            pltpu.VMEM((1, FULL), F32),
            pltpu.SemaphoreType.DMA((4,)),
            held(times, fields * snaps),
            held(times, SLOTS * snaps),
            held(ROWS),
            pltpu.VMEM((FULL, BLOCK * LANES), BF16),
            pltpu.VMEM((FULL, BLOCK * LANES), BF16),
            pltpu.VMEM((HALF, HALF), F32),
            pltpu.VMEM((HALF, HALF), F32),
            pltpu.VMEM((HALF, HALF), F32),
            held(2, chips, depth, tall, high),
            held(2, chips, depth, tall, high),
            held(chips, depth, tall, high),
            held(chips, depth, tall, part_a),
            held(depth, tall, part_a),
            held(tall, depth, part_a),
            held(depth, part_a),
            held(depth, part_a),
            held(tall, chips, depth, part_b),
            held(chips, depth, part_b),
            held(chips, depth, part_b),
            held(depth, part_b),
            held(depth, part_b),
            pltpu.SemaphoreType.DMA((times,)),
            pltpu.SemaphoreType.DMA((times,)),
            pltpu.SemaphoreType.DMA((8, most)),
            pltpu.SemaphoreType.DMA((8, most)),
        ],
        compiler_params=pltpu.CompilerParams(
            collective_id=0, has_side_effects=True, vmem_limit_bytes=64 << 20
        ),
    )(
        base_grid.reshape(fields * snaps, cells),
        index.reshape(chips, 1, 2 * LANES),
        exponents.T,
        codes,
    )


def solution(mesh):
    return jax.shard_map(
        shards,
        mesh=mesh,
        in_specs=(P(None, "tm", "pts"), P("pts"), P()),
        out_specs=(P("pts", "tm"), P(None, "pts")),
        check_vma=False,
    )
```
